256 devices in a mesh: section: 8 (over y, core), height: 32 (over z, x).
Axes of the slice: x: 4, y: 4, z: 8, core: 2. Of those that a mesh axis runs over, the one named last changes fastest.
Arguments:
- acts: bfloat16 [16, 1024, 2560], P(None, 'height'), may hold values from -7 to 7
- stale: bfloat16 [8, 16, 1024, 5120], P('section', None, 'height'), may hold values from -6 to 6
- layer_ids: int32 [8], P('section'), may hold values from 0 to 7, each once
- layer_gains: bfloat16 [8, 7680], replicated, may hold values from 0.25 to 4.5
- tile_lists: int32 [16, 32, 12], P(None, 'height'), may hold values from 0 to 47, as said below
- tile_counts: int32 [16, 32], P(None, 'height'), may hold values from 1 to 12, as said below
Outputs:
- latent_out: bfloat16 [16, 1024, 2560], P('section', 'height')
- kv_cache: bfloat16 [8, 16, 1024, 5120], P('section', None, 'height')
The draws below stay inside these ranges and needn't reach their ends.
Inputs may be any that keep to these rules, and one draw needn't show every extreme that they name: `tile_lists`: entry c names the key tile of patch c // 3 at tile height h + c % 3 - 1. The first tile_counts[p, h] entries are distinct, lie inside the grid, lie within 2 patches of p, and begin with the query tile itself, 3 p + 1. Entries after the count are other candidate numbers and are ignored. `tile_counts`: some query tile has all 12 entries live.
All inputs are finite; a program needn't handle non-finite values.
Results may differ from the reference program's by a relative error of at most 0.012.
Values may be sent and summed in bfloat16 or wider, within the bound.
No kernel may reach another device: no remote copies, remote signals or barrier semaphores. Data moves between devices by JAX's collectives and lax.ppermute only.
A program may use at most 128 MiB of HBM per device.

```python
import math
import jax
import jax.numpy as jnp
from jax import lax

HEADS = 20
HEAD_DIM = 128
TILE = 32
LIST = 12
REACH = 2
CH = 2560
PATCHES = 16
LAYERS = 8
ROWS = 1024
N_SECTION = 8
N_HEIGHT = 32


def tile_plan(key):
    key_one, key_two, key_three, key_four = jax.random.split(key, 4)
    patch_ids = jnp.arange(PATCHES, dtype=jnp.int32)[:, None, None]
    height_ids = jnp.arange(N_HEIGHT, dtype=jnp.int32)[None, :, None]
    candidate = jnp.arange(3 * PATCHES, dtype=jnp.int32)[None, None, :]
    source_patch = candidate // 3
    offset_side = candidate % 3
    target = height_ids + offset_side - 1
    inside = (jnp.abs(source_patch - patch_ids) <= REACH) & (target >= 0) & (target < N_HEIGHT)
    itself = (source_patch == patch_ids) & (offset_side == 1)
    jitter = jax.random.randint(key_one, (PATCHES, N_HEIGHT, 3 * PATCHES), 0, 1 << 16)
    rank_key = jnp.where(itself, 0, jnp.where(inside, 1, 2)) * (1 << 26) + jitter * 256 + candidate
    ranking = jnp.argsort(rank_key, axis=-1, stable=True).astype(jnp.int32)
    listed = ranking[:, :, :LIST]
    inside_count = jnp.sum(inside.astype(jnp.int32), axis=-1)
    dropped = jax.random.randint(key_two, (PATCHES, N_HEIGHT), 0, 4)
    keep_patch = jax.random.randint(key_three, (), 1, PATCHES - 2)
    keep_height = jax.random.randint(key_four, (), 1, N_HEIGHT - 1)
    marked = (jnp.arange(PATCHES, dtype=jnp.int32)[:, None] == keep_patch) & (jnp.arange(N_HEIGHT, dtype=jnp.int32)[None, :] == keep_height)
    dropped = jnp.where(marked, 0, dropped)
    counted = jnp.maximum(jnp.minimum(inside_count, LIST) - dropped, 1).astype(jnp.int32)
    return (listed, counted)


def draw_tile_lists(key, part):
    listed, counted = tile_plan(key)
    return listed


def draw_tile_counts(key, part):
    listed, counted = tile_plan(key)
    return counted


def log_range(key, shape, lower, upper):
    return jnp.exp(jax.random.uniform(key, shape, jnp.float32, jnp.log(lower), jnp.log(upper)))


def draw_layer_gains(key, part):
    key = jax.random.fold_in(key, 11)
    key_one, key_two = jax.random.split(key, 2)
    pair_gains = log_range(key_one, (LAYERS, 2 * CH), 0.25, 1.0)
    value_gains = log_range(key_two, (LAYERS, CH), 0.25, 1.0)
    return jnp.concatenate([pair_gains, value_gains], axis=1).astype(jnp.bfloat16)


def draw_acts(key, part):
    key = jax.random.fold_in(key, 7)
    key_one = jax.random.fold_in(key, 0)
    return jnp.clip(jax.random.normal(key_one, (PATCHES, ROWS, CH), jnp.float32), -6.0, 6.0).astype(jnp.bfloat16)


def block_levels(key, shape, cuts, smallest, high):
    def one(dim, shards_of):
        steps = jax.random.uniform(jax.random.fold_in(jax.random.fold_in(key, 6), dim), (shards_of,), jnp.float32, smallest / len(cuts), high / len(cuts))
        return jnp.repeat(jnp.exp(steps), shape[dim] // shards_of).reshape((-1,) + (1,) * (len(shape) - dim - 1))

    loudness = one(*cuts[0])
    for cut in cuts[1:]:
        loudness = loudness * one(*cut)
    return loudness


def noise(stream_key, dims, width, reach, cuts=(), held_as=jnp.bfloat16):
    gain = block_levels(stream_key, dims, cuts, -0.22, 0.18) if cuts else 1.0
    result = jax.random.normal(stream_key, dims, jnp.float32) * width * gain
    return jnp.minimum(jnp.maximum(result, -reach), reach).astype(held_as)


def setup_inputs(seed: int = 0) -> dict:
    key_list = jax.random.split(jax.random.key(seed), 7)
    acts = draw_acts(jax.random.fold_in(key_list[6], 71), 0)
    stale = noise(key_list[1], (N_SECTION, PATCHES, ROWS, 2 * CH), 1.0, 6.0, ((0, 8), (2, 32)))
    layer_ids = jax.random.permutation(key_list[2], LAYERS).astype(jnp.int32)
    layer_gains = draw_layer_gains(jax.random.fold_in(key_list[6], 71), 0)
    tile_lists = draw_tile_lists(jax.random.fold_in(key_list[6], 71), 0)
    tile_counts = draw_tile_counts(jax.random.fold_in(key_list[6], 71), 0)
    return dict(acts=acts, stale=stale, layer_ids=layer_ids, layer_gains=layer_gains, tile_lists=tile_lists, tile_counts=tile_counts)


def normalize(rows):
    return rows / jnp.sqrt(lax.optimization_barrier(jnp.mean(rows * rows, axis=-1, keepdims=True)) + 1e-06)

def reference(acts, stale, layer_ids, layer_gains, tile_lists, tile_counts):
    tiles_high = ROWS // TILE
    section_total = stale.shape[0]
    factor = 1.0 / math.sqrt(HEAD_DIM)
    current = acts
    caches = []
    for section_now in range(section_total):
        selector = (jnp.arange(LAYERS, dtype=jnp.int32) == layer_ids[section_now]).astype(jnp.float32)
        gain_row = jnp.dot(selector, layer_gains.astype(jnp.float32), precision=lax.Precision.HIGHEST)
        gain_query = gain_row[:CH]
        gain_key = gain_row[CH:2 * CH]
        gain_value = gain_row[2 * CH:]
        buffer = stale[section_now].reshape(PATCHES, tiles_high, TILE, 2 * CH)
        produced = []
        for patch_now in range(PATCHES):
            inputs = current[patch_now].astype(jnp.float32)
            normed = normalize(inputs)
            fresh_pairs = jnp.concatenate([normed * gain_key, normed * gain_value], axis=-1).astype(jnp.bfloat16)
            buffer = buffer.at[patch_now].set(fresh_pairs.reshape(tiles_high, TILE, 2 * CH))
            queries = (normed * gain_query).astype(jnp.bfloat16).reshape(tiles_high, TILE, HEADS, HEAD_DIM)
            padded = jnp.pad(buffer, ((0, 0), (1, 1), (0, 0), (0, 0)))
            chosen = tile_lists[patch_now].astype(jnp.int32)
            source = chosen // 3
            height_pos = jnp.arange(tiles_high, dtype=jnp.int32)[:, None] + chosen % 3
            gathered = padded[source, height_pos].reshape(tiles_high, LIST * TILE, 2, HEADS, HEAD_DIM)
            living = jnp.repeat(jnp.arange(LIST, dtype=jnp.int32)[None, :] < tile_counts[patch_now][:, None], TILE, axis=1)
            scores = jnp.einsum('nqhd,nkhd->nhqk', queries.astype(jnp.float32), gathered[:, :, 0].astype(jnp.float32)) * factor
            scores = jnp.where(living[:, None, None, :], scores, -1e+30)
            highest = lax.optimization_barrier(jnp.max(scores, axis=-1, keepdims=True))
            exponent = jnp.exp(scores - highest)
            weights = (exponent / lax.optimization_barrier(jnp.sum(exponent, axis=-1, keepdims=True))).astype(jnp.bfloat16)
            attended = jnp.einsum('nhqk,nkhd->nqhd', weights.astype(jnp.float32), gathered[:, :, 1].astype(jnp.float32))
            produced.append((inputs + attended.reshape(ROWS, CH)).astype(jnp.bfloat16))
        current = jnp.stack(produced)
        caches.append(buffer.reshape(PATCHES, ROWS, 2 * CH))
    return (current, jnp.stack(caches))
```

```python
import functools
import math

import jax
import jax.numpy as jnp
from jax import lax
from jax.experimental import pallas as pl
from jax.experimental.pallas import tpu as pltpu
from jax.sharding import PartitionSpec as P

HEAD_DIM = 128
BLOCK = 2
PAIR = 2 * HEAD_DIM
SCALE = 1.0 / math.sqrt(HEAD_DIM)
NEVER = -1e30
VMEM = 56 * 1024 * 1024


def normalized(tile):
    wide = tile.astype(jnp.float32)
    return wide * (1.0 / jnp.sqrt(jnp.mean(wide * wide, axis=-1, keepdims=True) + 1e-06))


def split_heads(pair):
    zeros = jnp.zeros((pair.shape[0], HEAD_DIM), pair.dtype)
    return jnp.concatenate(
        [
            jnp.concatenate([pair[:, :HEAD_DIM], zeros], axis=1),
            jnp.concatenate([zeros, pair[:, HEAD_DIM:]], axis=1),
        ],
        axis=0,
    )


def joined_heads(both):
    rows = both.shape[0] // 2
    return jnp.concatenate([both[:rows, :HEAD_DIM], both[rows:, HEAD_DIM:]], axis=1)


def products(queries, keys):
    return lax.dot_general(
        queries, keys, (((1,), (1,)), ((), ())), preferred_element_type=jnp.float32
    )


def pairs_of(normed, gains_ref):
    channels = normed.shape[-1]
    return (
        (normed * gains_ref[:, channels : 2 * channels]).astype(jnp.bfloat16),
        (normed * gains_ref[:, 2 * channels :]).astype(jnp.bfloat16),
    )


def own_kernel(
    where_ref,
    self_ref,
    past_low,
    old_own,
    past_high,
    next_own,
    second_own,
    third_own,
    next_low,
    next_high,
    later_low,
    later_high,
    gains_ref,
    bias_even,
    bias_odd,
    cache_in,
    queries_ref,
    fresh_ref,
    mixed_ref,
    highest_ref,
    total_ref,
    cache_ref,
    sent,
    old_low,
    old_high,
    even_scores,
    odd_scores,
    even_weights,
    odd_weights,
):
    del cache_in
    channels = self_ref.shape[-1]
    pairs = channels // PAIR
    active = where_ref[1] > 0

    @pl.when(active)
    def _():
        for i in range(BLOCK):
            normed = normalized(self_ref[i])
            queries_ref[i] = (normed * gains_ref[:, :channels]).astype(jnp.bfloat16)
            fresh_ref[i, :, :channels], fresh_ref[i, :, channels:] = pairs_of(normed, gains_ref)
        writing = pltpu.make_async_copy(
            fresh_ref, cache_ref.at[pl.ds(where_ref[0] * BLOCK, BLOCK)], sent
        )
        writing.start()
        for past, old in ((past_low, old_low), (past_high, old_high)):
            for i in range(BLOCK):
                normed = normalized(past[i])
                old[i, :, :channels], old[i, :, channels:] = pairs_of(normed, gains_ref)

        def tiles_of(i, cut):
            old = [ref[j, :, cut] for j in range(i, BLOCK) for ref in (old_low, old_own, old_high)]
            fresh = [fresh_ref[j, :, cut] for j in range(i + 1)]
            near = [next_low[0, :, cut], next_own[0, :, cut], next_high[0, :, cut]]
            second = [later_low[0, :, cut], second_own[0, :, cut], later_high[0, :, cut]]
            third = [later_low[1, :, cut], third_own[0, :, cut], later_high[1, :, cut]]
            return jnp.concatenate(
                old + fresh + (near + second if i == 0 else second + third), axis=0
            )

        sides = ((even_scores, even_weights, bias_even), (odd_scores, odd_weights, bias_odd))
        for pair in range(pairs):
            cut = slice(pair * PAIR, (pair + 1) * PAIR)
            for i, (scores_ref, _, _) in enumerate(sides):
                scores_ref[pair] = products(
                    split_heads(queries_ref[i, :, cut]), tiles_of(i, cut)
                )
        for pair in range(pairs):
            for i, (scores_ref, weights_ref, bias) in enumerate(sides):
                scores = scores_ref[pair] * SCALE + bias[0]
                highest = jnp.max(scores, axis=-1, keepdims=True)
                exponent = jnp.exp(scores - highest)
                highest_ref[i, :, pair : pair + 1] = highest
                total_ref[i, :, pair : pair + 1] = jnp.sum(exponent, axis=-1, keepdims=True)
                weights_ref[pair] = exponent.astype(jnp.bfloat16)
        for pair in range(pairs):
            cut = slice(pair * PAIR, (pair + 1) * PAIR)
            value_cut = slice(channels + pair * PAIR, channels + (pair + 1) * PAIR)
            for i, (_, weights_ref, _) in enumerate(sides):
                mixed_ref[i, :, cut] = joined_heads(
                    jnp.dot(
                        weights_ref[pair],
                        tiles_of(i, value_cut),
                        preferred_element_type=jnp.float32,
                    )
                )
        writing.wait()

    @pl.when(jnp.logical_not(active))
    def _():
        fresh_ref[...] = jnp.zeros_like(fresh_ref)


def side_kernel(where_ref, *refs, relayed):
    (
        self_ref,
        low_ref,
        high_ref,
        queries_ref,
        mixed_ref,
        highest_ref,
        total_ref,
        gains_ref,
        bias_ref,
    ) = refs[:9]
    entering_ref = refs[9] if relayed else None
    result_ref, keys, values, scores_ref, weights_ref, shrink_ref = refs[-6:]
    channels = self_ref.shape[-1]
    rows = self_ref.shape[1]
    pairs = channels // PAIR
    active = where_ref[1] > 0
    last = where_ref[2] > 0

    @pl.when(active)
    def _():
        for side, source in enumerate((low_ref, high_ref)):
            for i in range(BLOCK):
                at = pl.ds((side * BLOCK + i) * rows, rows)
                keys[at, :], values[at, :] = pairs_of(normalized(source[i]), gains_ref)
        bias = jnp.concatenate(
            [
                jnp.broadcast_to(bias_ref[0, i : i + 1], (2 * rows, bias_ref.shape[-1]))
                for i in range(BLOCK)
            ],
            axis=0,
        )
        for pair in range(pairs):
            cut = slice(pair * PAIR, (pair + 1) * PAIR)
            both = jnp.concatenate(
                [split_heads(queries_ref[i, :, cut]) for i in range(BLOCK)], axis=0
            )
            scores_ref[pair] = products(both, keys[:, cut])
        for pair in range(pairs):
            scores = scores_ref[pair] * SCALE + bias
            column = slice(pair, pair + 1)
            before = jnp.concatenate([highest_ref[i, :, column] for i in range(BLOCK)], axis=0)
            sums = jnp.concatenate([total_ref[i, :, column] for i in range(BLOCK)], axis=0)
            highest = jnp.maximum(before, jnp.max(scores, axis=-1, keepdims=True))
            exponent = jnp.exp(scores - highest)
            shrink = jnp.exp(before - highest)
            inverse = 1.0 / (sums * shrink + jnp.sum(exponent, axis=-1, keepdims=True))
            weights_ref[pair] = (exponent * inverse).astype(jnp.bfloat16)
            shrink_ref[pair] = jnp.broadcast_to(shrink * inverse, (BLOCK * 2 * rows, HEAD_DIM))
        for pair in range(pairs):
            cut = slice(pair * PAIR, (pair + 1) * PAIR)
            added = jnp.dot(
                weights_ref[pair], values[:, cut], preferred_element_type=jnp.float32
            )
            shrink = shrink_ref[pair]
            for i in range(BLOCK):
                top = 2 * rows * i
                kept = mixed_ref[i, :, cut] * jnp.concatenate(
                    [shrink[top : top + rows], shrink[top + rows : top + 2 * rows]], axis=1
                )
                result_ref[i, :, cut] = (
                    self_ref[i, :, cut].astype(jnp.float32)
                    + kept
                    + joined_heads(added[top : top + 2 * rows])
                ).astype(jnp.bfloat16)

    if relayed:

        @pl.when(last)
        def _():
            result_ref[...] = entering_ref[...]

    @pl.when(jnp.logical_not(active | last) if relayed else jnp.logical_not(active))
    def _():
        result_ref[...] = jnp.zeros_like(result_ref)


def whole(shape):
    return pl.BlockSpec(shape, lambda i, w: (0,) * len(shape))


def at_block(shape):
    return pl.BlockSpec((1,) + shape, lambda i, w: (w[0],) + (0,) * len(shape))


def own_part(where, tile, old, stale, near, far, gains, biases, cache):
    patches, rows, pair_channels = stale.shape
    channels = pair_channels // 2

    def at_patch(shift):
        return pl.BlockSpec(
            (1, rows, pair_channels),
            lambda i, w: (jnp.minimum(w[0] * BLOCK + shift, patches - 1), 0, 0),
        )

    pairs = whole((BLOCK, rows, pair_channels))
    block = whole((BLOCK, rows, channels))
    stats = whole((BLOCK, 2 * rows, HEAD_DIM))
    second = pl.BlockSpec((1, rows, pair_channels), lambda i, w: (1, 0, 0))
    even, odd = biases[0].shape[-1], biases[1].shape[-1]
    count = channels // PAIR
    return pl.pallas_call(
        own_kernel,
        grid_spec=pltpu.PrefetchScalarGridSpec(
            num_scalar_prefetch=1,
            grid=(1,),
            in_specs=[block, block, pairs, block]
            + [at_patch(1), at_patch(2), at_patch(3)]
            + [second, second, pairs, pairs]
            + [whole(gains.shape), at_block((1, even)), at_block((1, odd))]
            + [pl.BlockSpec(memory_space=pl.ANY)],
            out_specs=[block, pairs, block, stats, stats, pl.BlockSpec(memory_space=pl.ANY)],
            scratch_shapes=[
                pltpu.SemaphoreType.DMA,
                pltpu.VMEM((BLOCK, rows, pair_channels), jnp.bfloat16),
                pltpu.VMEM((BLOCK, rows, pair_channels), jnp.bfloat16),
                pltpu.VMEM((count, 2 * rows, even), jnp.float32),
                pltpu.VMEM((count, 2 * rows, odd), jnp.float32),
                pltpu.VMEM((count, 2 * rows, even), jnp.bfloat16),
                pltpu.VMEM((count, 2 * rows, odd), jnp.bfloat16),
            ],
        ),
        out_shape=[
            jax.ShapeDtypeStruct((BLOCK, rows, channels), jnp.bfloat16),
            jax.ShapeDtypeStruct((BLOCK, rows, pair_channels), jnp.bfloat16),
            jax.ShapeDtypeStruct((BLOCK, rows, channels), jnp.float32),
            jax.ShapeDtypeStruct((BLOCK, 2 * rows, HEAD_DIM), jnp.float32),
            jax.ShapeDtypeStruct((BLOCK, 2 * rows, HEAD_DIM), jnp.float32),
            jax.ShapeDtypeStruct(cache.shape, jnp.bfloat16),
        ],
        input_output_aliases={15: 5},
        compiler_params=pltpu.CompilerParams(vmem_limit_bytes=VMEM),
        cost_estimate=pl.CostEstimate(
            flops=8 * rows * (even + odd) * channels, bytes_accessed=16000000, transcendentals=0
        ),
    )(where, tile, *old, stale, stale, stale, near[0], near[1], far[0], far[1], gains, *biases, cache)


def side_part(where, tile, low, high, queries, mixed, highest, total, gains, bias, entering):
    rows, channels = tile.shape[1:]
    block = whole((BLOCK, rows, channels))
    stats = whole((BLOCK, 2 * rows, HEAD_DIM))
    keys = bias.shape[-1]
    count = channels // PAIR
    relayed = entering is not None
    return pl.pallas_call(
        functools.partial(side_kernel, relayed=relayed),
        grid_spec=pltpu.PrefetchScalarGridSpec(
            num_scalar_prefetch=1,
            grid=(1,),
            in_specs=[block] * 5
            + [stats] * 2
            + [whole(gains.shape), at_block((BLOCK, keys))]
            + [block] * relayed,
            out_specs=block,
            scratch_shapes=[
                pltpu.VMEM((keys, channels), jnp.bfloat16),
                pltpu.VMEM((keys, channels), jnp.bfloat16),
                pltpu.VMEM((count, 2 * BLOCK * rows, keys), jnp.float32),
                pltpu.VMEM((count, 2 * BLOCK * rows, keys), jnp.bfloat16),
                pltpu.VMEM((count, 2 * BLOCK * rows, HEAD_DIM), jnp.float32),
            ],
        ),
        out_shape=jax.ShapeDtypeStruct((BLOCK, rows, channels), jnp.bfloat16),
        compiler_params=pltpu.CompilerParams(vmem_limit_bytes=VMEM),
        cost_estimate=pl.CostEstimate(
            flops=16 * rows * keys * channels, bytes_accessed=6000000, transcendentals=0
        ),
    )(
        where, tile, low, high, queries, mixed, highest, total, gains, bias,
        *([entering] if relayed else []),
    )


def hop(value, section_shift, height_shift):
    sections, heights = lax.axis_size("section"), lax.axis_size("height")
    pairs = [
        (
            s * heights + h,
            (s + section_shift) % sections * heights + (h + height_shift) % heights,
        )
        for s in range(sections)
        for h in range(heights)
    ]
    return lax.ppermute(value, ("section", "height"), pairs)


def swapped(value, one, other):
    pairs = [(s, s) for s in range(lax.axis_size("section")) if s not in (one, other)]
    return lax.ppermute(value, "section", pairs + [(one, other), (other, one)])


def key_biases(tile_lists, tile_counts, rows):
    lists = tile_lists[:, 0, :]
    patches = lists.shape[0]
    live = jnp.arange(lists.shape[1], dtype=jnp.int32)[None, :] < tile_counts
    wanted = (
        3 * (jnp.arange(patches, dtype=jnp.int32) - 2)[:, None]
        + jnp.arange(15, dtype=jnp.int32)[None, :]
    )
    listed = jnp.any((lists[:, :, None] == wanted[:, None, :]) & live[:, :, None], axis=1)
    listed = listed.reshape(patches // BLOCK, BLOCK, 15)

    def bias(i, columns):
        chosen = jnp.stack(
            [listed[:, i, c] if c >= 0 else jnp.zeros_like(listed[:, i, 0]) for c in columns], axis=1
        )
        chosen = jnp.repeat(chosen, rows, axis=1)
        return jnp.where(chosen, 0.0, NEVER).astype(jnp.float32)[:, None, :]

    even = bias(0, (0, 1, 2, 3, 4, 5, 7, 9, 10, 11, 12, 13, 14))
    odd = bias(1, (0, 1, 2, 4, 7, 9, 10, 11, 12, 13, 14))
    side = jnp.concatenate([bias(0, (6, -1, 8, -1)), bias(1, (3, 6, 5, 8))], axis=1)
    return (even, odd), side


def body(acts, stale, layer_ids, layer_gains, tile_lists, tile_counts):
    sections = lax.axis_size("section")
    position = lax.axis_index("section")
    patches, rows, channels = acts.shape
    blocks = patches // BLOCK
    stale = stale[0]
    gains = lax.dynamic_slice_in_dim(layer_gains, layer_ids[0], 1, 0).astype(jnp.float32)
    biases, side_bias = key_biases(tile_lists, tile_counts, rows)
    acts = acts.reshape(blocks, BLOCK, rows, channels)

    def halo_of(moment, after=None):
        first = BLOCK * (moment - position + 1)
        if after is not None:
            first, _ = lax.optimization_barrier((first, after))
        sent = lax.dynamic_slice_in_dim(stale, jnp.clip(first, 0, patches - BLOCK), BLOCK, 0)
        return [hop(sent, 0, 1), hop(sent, 0, -1)]

    def relay(payload):
        return [hop(payload, 1, shift) for shift in (0, 1, -1)]

    moments = blocks + sections - 1
    own = jnp.zeros((BLOCK, rows, 2 * channels), jnp.bfloat16)
    past_low = past_high = jnp.zeros((BLOCK, rows, channels), jnp.bfloat16)
    cache = jnp.zeros(stale.shape, jnp.bfloat16)
    tile, low, high = relay(acts[0])
    halos = [halo_of(-1), halo_of(0), halo_of(1)]
    latent = None
    for moment in range(moments):
        block = moment - position
        where = jnp.stack(
            [
                jnp.clip(block, 0, blocks - 1),
                ((block >= 0) & (block < blocks)).astype(jnp.int32),
                (position == sections - 1).astype(jnp.int32),
            ]
        )
        queries, own, mixed, highest, total, cache = own_part(
            where,
            tile,
            (past_low, own, past_high),
            stale,
            halos[moment],
            halos[moment + 1],
            gains,
            biases,
            cache,
        )
        entering = acts[moment + 1] if moment + 1 < blocks else None
        result = side_part(
            where, tile, low, high, queries, mixed, highest, total, gains, side_bias, entering
        )
        past_low, past_high = low, high
        if moment + 1 < moments:
            tile, low, high = relay(result)
            if moment + 2 < moments - 1:
                halos.append(halo_of(moment + 2, result[0, 0, 0]))
            else:
                halos.append(halos[-1])
        owner = moment - (sections - 1)
        if owner >= 0:
            arrived = swapped(result, sections - 1, owner) if owner < sections - 1 else result
            latent = arrived if latent is None else jnp.where(position == owner, arrived, latent)
    return (latent, cache[None])


def solution(mesh):
    return jax.shard_map(
        body,
        mesh=mesh,
        in_specs=(
            P(None, "height", None),
            P("section", None, "height", None),
            P("section"),
            P(),
            P(None, "height", None),
            P(None, "height"),
        ),
        out_specs=(P("section", "height", None), P("section", None, "height", None)),
        check_vma=False,
    )
```

```python
import functools
import math

import jax
import jax.numpy as jnp
from jax import lax
from jax.experimental import pallas as pl
from jax.experimental.pallas import tpu as pltpu
from jax.sharding import PartitionSpec as P

HEAD_DIM = 128
PAIR = 2 * HEAD_DIM
SCALE = 1.0 / math.sqrt(HEAD_DIM)
NEVER = -1e30
WINDOW = 5
BLOCK = 2
VMEM = 60 * 1024 * 1024
OUTSIDE = pl.BlockSpec(memory_space=pltpu.HBM)
SCALARS = pl.BlockSpec(memory_space=pltpu.SMEM)
PIECES = ((1, 4), (4, 6), (6, 8), (8, 10), (10, 12), (12, 14), (14, 16))
SENT_AT = (-1, 0, 1, 2, 3, 4, 5)


def normalized(tile):
    wide = tile.astype(jnp.float32)
    return wide / jnp.sqrt(jnp.mean(wide * wide, axis=-1, keepdims=True) + 1e-06)


def split_heads(pair):
    zeros = jnp.zeros((pair.shape[0], HEAD_DIM), pair.dtype)
    return jnp.concatenate(
        [
            jnp.concatenate([pair[:, :HEAD_DIM], zeros], axis=1),
            jnp.concatenate([zeros, pair[:, HEAD_DIM:]], axis=1),
        ],
        axis=0,
    )


def joined_heads(both):
    rows = both.shape[0] // 2
    return jnp.concatenate([both[:rows, :HEAD_DIM], both[rows:, HEAD_DIM:]], axis=1)


def step_kernel(where_ref, *refs, pieces, relayed):
    tiles_hbm, (gains_hbm, bias_hbm, past_low, past_high, _) = refs[:3], refs[3:8]
    lows, highs = refs[8 : 8 + pieces], refs[8 + pieces : 8 + 2 * pieces]
    entering_hbm = refs[8 + 2 * pieces] if relayed else None
    (
        result_hbm,
        next_low,
        next_high,
        cache_ref,
        ready,
        sent,
        arrived,
        recalled,
        gains_ref,
        bias_ref,
        tiles,
        old_ref,
        fresh_ref,
        later_ref,
        queries,
        scores_ref,
        weights_ref,
        result_ref,
    ) = refs[8 + 2 * pieces + relayed :]
    sending = jnp.logical_not(where_ref[2] > 0) if relayed else where_ref[1] > 0
    rows, channels = tiles.shape[2:]
    pairs = channels // PAIR
    block, active, last = where_ref[0], where_ref[1] > 0, where_ref[2] > 0
    here = pl.ds(block * BLOCK, BLOCK)
    before = pl.ds(jnp.maximum(block - 1, 0) * BLOCK, BLOCK)
    reading = [
        pltpu.make_async_copy(source, target, ready.at[n])
        for n, (source, target) in enumerate(
            [(gains_hbm, gains_ref), (bias_hbm.at[block], bias_ref)]
            + [(tiles_hbm[side], tiles.at[side]) for side in range(3)]
        )
    ]
    writing = [
        pltpu.make_async_copy(fresh_ref.at[n], target, sent.at[n])
        for n, target in enumerate((next_low, cache_ref.at[here], next_high))
    ]
    half = channels // 2
    leaving = [
        pltpu.make_async_copy(
            result_ref.at[:, :, pl.ds(n * half, half)],
            result_hbm.at[:, :, pl.ds(n * half, half)],
            sent.at[3 + n],
        )
        for n in range(2)
    ]

    recalls = [
        pltpu.make_async_copy(source, old_ref.at[side], recalled.at[side])
        for side, source in enumerate((past_low, cache_ref.at[before], past_high))
    ]

    def coming(side, source, first, end):
        return pltpu.make_async_copy(
            source, later_ref.at[side, pl.ds(first, end - first)], arrived.at[side, first]
        )

    def own_ahead(count):
        return coming(1, cache_ref.at[pl.ds(block * BLOCK + 1, count)], 0, count)

    @pl.when(active)
    def _():
        for copy in reading:
            copy.start()
        for n in range(pieces):

            @pl.when(block == n)
            def _():
                own_ahead(3).start()
                for side, mine in ((0, lows), (2, highs)):
                    if n == 0:
                        coming(side, mine[0], 0, 3).start()
                    else:
                        final = mine[n - 1].shape[0] - 1
                        coming(side, mine[n - 1].at[pl.ds(final, 1)], 0, 1).start()
                        coming(side, mine[n], 1, 3).start()

        if pieces == len(PIECES):

            @pl.when(block == pieces)
            def _():
                own_ahead(1).start()
                for side, mine in ((0, lows), (2, highs)):
                    coming(side, mine[-1].at[pl.ds(1, 1)], 0, 1).start()
                later_ref[:, 1:] = jnp.zeros_like(later_ref[:, 1:])

        @pl.when(block > 0)
        def _():
            for copy in recalls:
                copy.start()

        @pl.when(block == 0)
        def _():
            old_ref[...] = jnp.zeros_like(old_ref)

        for copy in reading:
            copy.wait()
        for side in range(3):
            for i in range(BLOCK):
                normed = normalized(tiles[side, i])
                fresh_ref[side, i, :, :channels] = (
                    normed * gains_ref[:, channels : 2 * channels]
                ).astype(jnp.bfloat16)
                fresh_ref[side, i, :, channels:] = (normed * gains_ref[:, 2 * channels :]).astype(
                    jnp.bfloat16
                )
                if side == 1:
                    queries[i] = (normed * gains_ref[:, :channels]).astype(jnp.bfloat16)
        some = later_ref.at[0]

        @pl.when(block < len(PIECES))
        def _():
            own_ahead(3).wait()

        @pl.when(block == len(PIECES))
        def _():
            own_ahead(1).wait()

        @pl.when(block == 0)
        def _():
            for side in (0, 2):
                coming(side, some, 0, 3).wait()

        @pl.when(block > 0)
        def _():
            for side in (0, 2):
                coming(side, some.at[pl.ds(0, 1)], 0, 1).wait()
            for copy in recalls:
                copy.wait()

        @pl.when((block > 0) & (block < len(PIECES)))
        def _():
            for side in (0, 2):
                coming(side, some.at[pl.ds(1, 2)], 1, 3).wait()

        for copy in writing:
            copy.start()

        def tiles_of(i, cut):
            old = [old_ref[side, j, :, cut] for j in range(i, BLOCK) for side in range(3)]
            fresh = [fresh_ref[side, j, :, cut] for j in range(i + 1) for side in range(3)]
            later = [later_ref[side, ahead, :, cut] for ahead in (i, i + 1) for side in range(3)]
            return jnp.concatenate(old + fresh + later, axis=0)

        for pair in range(pairs):
            cut = slice(pair * PAIR, (pair + 1) * PAIR)
            for i in range(BLOCK):
                scores_ref[i, pair] = lax.dot_general(
                    split_heads(queries[i, :, cut]),
                    tiles_of(i, cut),
                    (((1,), (1,)), ((), ())),
                    preferred_element_type=jnp.float32,
                )
        for pair in range(pairs):
            for i in range(BLOCK):
                scores = scores_ref[i, pair] * SCALE + bias_ref[i : i + 1]
                exponent = jnp.exp(scores - jnp.max(scores, axis=-1, keepdims=True))
                total = jnp.sum(exponent, axis=-1, keepdims=True)
                weights_ref[i, pair] = (exponent * (1.0 / total)).astype(jnp.bfloat16)
        for pair in range(pairs):
            cut = slice(pair * PAIR, (pair + 1) * PAIR)
            value_cut = slice(channels + pair * PAIR, channels + (pair + 1) * PAIR)
            for i in range(BLOCK):
                mixed = jnp.dot(
                    weights_ref[i, pair], tiles_of(i, value_cut), preferred_element_type=jnp.float32
                )
                result_ref[i, :, cut] = (
                    tiles[1, i, :, cut].astype(jnp.float32) + joined_heads(mixed)
                ).astype(jnp.bfloat16)
            if pair == pairs // 2 - 1:

                @pl.when(sending)
                def _():
                    leaving[0].start()

        @pl.when(sending)
        def _():
            leaving[1].start()
            for copy in leaving:
                copy.wait()

        for copy in writing:
            copy.wait()

    if relayed:

        @pl.when(last)
        def _():
            entering = pltpu.make_async_copy(entering_hbm, result_hbm, ready.at[0])
            entering.start()
            entering.wait()


def step(where, tiles, past, gains, bias, cache, halos, entering):
    patches, rows, pair_channels = cache.shape
    channels = pair_channels // 2
    keys = bias.shape[-1]
    pairs = channels // PAIR
    relayed = entering is not None
    side = jax.ShapeDtypeStruct((BLOCK, rows, pair_channels), jnp.bfloat16)
    return pl.pallas_call(
        functools.partial(step_kernel, pieces=len(halos), relayed=relayed),
        in_specs=[SCALARS] + [OUTSIDE] * (8 + 2 * len(halos) + relayed),
        out_specs=[OUTSIDE] * 4,
        scratch_shapes=[
            pltpu.SemaphoreType.DMA((5,)),
            pltpu.SemaphoreType.DMA((5,)),
            pltpu.SemaphoreType.DMA((3, 2)),
            pltpu.SemaphoreType.DMA((3,)),
            pltpu.VMEM(gains.shape, jnp.float32),
            pltpu.VMEM((BLOCK, keys), jnp.float32),
            pltpu.VMEM((3, BLOCK, rows, channels), jnp.bfloat16),
            pltpu.VMEM((3, BLOCK, rows, pair_channels), jnp.bfloat16),
            pltpu.VMEM((3, BLOCK, rows, pair_channels), jnp.bfloat16),
            pltpu.VMEM((3, 3, rows, pair_channels), jnp.bfloat16),
            pltpu.VMEM((BLOCK, rows, channels), jnp.bfloat16),
            pltpu.VMEM((BLOCK, pairs, 2 * rows, keys), jnp.float32),
            pltpu.VMEM((BLOCK, pairs, 2 * rows, keys), jnp.bfloat16),
            pltpu.VMEM((BLOCK, rows, channels), jnp.bfloat16),
        ],
        out_shape=[
            jax.ShapeDtypeStruct((BLOCK, rows, channels), jnp.bfloat16),
            side,
            side,
            jax.ShapeDtypeStruct(cache.shape, jnp.bfloat16),
        ],
        input_output_aliases={8: 3},
        compiler_params=pltpu.CompilerParams(vmem_limit_bytes=VMEM),
        cost_estimate=pl.CostEstimate(
            flops=8 * BLOCK * rows * keys * channels, bytes_accessed=12000000, transcendentals=0
        ),
    )(
        where, *tiles, gains, bias, *past, cache,
        *[low for low, _ in halos], *[high for _, high in halos],
        *([entering] if relayed else []),
    )


def hop(value, section_shift, height_shift):
    sections, heights = lax.axis_size("section"), lax.axis_size("height")
    pairs = [
        (
            s * heights + h,
            (s + section_shift) % sections * heights + (h + height_shift) % heights,
        )
        for s in range(sections)
        for h in range(heights)
    ]
    return lax.ppermute(value, ("section", "height"), pairs)


def nothing_of(value):
    return jnp.where(value.astype(jnp.int32) == 123456789, 1, 0)


def relay(payload):
    low, high = hop(payload, 1, 1), hop(payload, 1, -1)
    return low, hop(payload, 1, 0), high


def swapped(value, one, other):
    pairs = [(s, s) for s in range(lax.axis_size("section")) if s not in (one, other)]
    return lax.ppermute(value, "section", pairs + [(one, other), (other, one)])


def key_bias(tile_lists, tile_counts, rows):
    lists = tile_lists[:, 0, :]
    patches = lists.shape[0]
    live = jnp.arange(lists.shape[1], dtype=jnp.int32)[None, :] < tile_counts
    wanted = (
        3 * (jnp.arange(patches, dtype=jnp.int32) - WINDOW // 2)[:, None]
        + jnp.arange(3 * WINDOW, dtype=jnp.int32)[None, :]
    )
    listed = jnp.any((lists[:, :, None] == wanted[:, None, :]) & live[:, :, None], axis=1)
    listed = jnp.repeat(listed, rows, axis=1)
    bias = jnp.where(listed, 0.0, NEVER).astype(jnp.float32)
    return bias.reshape(patches // BLOCK, BLOCK, bias.shape[-1])


def body(acts, stale, layer_ids, layer_gains, tile_lists, tile_counts):
    sections = lax.axis_size("section")
    position = lax.axis_index("section")
    patches, rows, channels = acts.shape
    stale = stale[0]

    def halo_of(piece, after):
        sent = stale[piece[0] : piece[1]]
        if after is not None:
            first = piece[0] + nothing_of(after)
            sent = lax.dynamic_slice_in_dim(stale, first, piece[1] - piece[0], axis=0)
        return hop(sent, 0, 1), hop(sent, 0, -1)

    blocks = patches // BLOCK
    acts = acts.reshape(blocks, BLOCK, rows, channels)
    tiles = relay(acts[0])
    halos = [halo_of(piece, None) for piece, at in zip(PIECES, SENT_AT) if at < 0]
    gains = lax.dynamic_slice_in_dim(layer_gains, layer_ids[0], 1, 0).astype(jnp.float32)
    bias = key_bias(tile_lists, tile_counts, rows)
    moments = blocks + sections - 1
    past = [jnp.zeros((BLOCK, rows, 2 * channels), jnp.bfloat16)] * 2
    cache = stale
    latent = None
    for moment in range(moments):
        block = moment - position
        where = jnp.stack(
            [
                jnp.clip(block, 0, blocks - 1),
                ((block >= 0) & (block < blocks)).astype(jnp.int32),
                (position == sections - 1).astype(jnp.int32),
            ]
        )
        ready = [halo for halo, (first, _) in zip(halos, PIECES) if first <= BLOCK * moment + 3]
        entering = acts[moment + 1] if moment + 1 < blocks else None
        for piece, at in zip(PIECES, SENT_AT):
            if at == moment:
                halos.append(halo_of(piece, halos[0][1][0, 0, 0] if moment == 0 else None))
        result, *past, cache = step(where, tiles, past, gains, bias, cache, ready, entering)
        if moment + 1 < moments:
            tiles = relay(result)
        owner = moment - (sections - 1)
        if owner >= 0:
            arrived = swapped(result, sections - 1, owner) if owner < sections - 1 else result
            latent = arrived if latent is None else jnp.where(position == owner, arrived, latent)
    return (latent, cache[None])


def solution(mesh):
    return jax.shard_map(
        body,
        mesh=mesh,
        in_specs=(
            P(None, "height", None),
            P("section", None, "height", None),
            P("section"),
            P(),
            P(None, "height", None),
            P(None, "height"),
        ),
        out_specs=(P("section", "height", None), P("section", None, "height", None)),
        check_vma=False,
    )
```
